32 devices in a mesh: slab: 16 (over z, x, core), grp: 2 (over y).
Axes of the slice: x: 2, y: 2, z: 4, core: 2. Of those that a mesh axis runs over, the one named last changes fastest.
Arguments:
- adj_out: float32 [5, 128, 64, 256], P(None, 'grp', 'slab'), may hold values from -6 to 6
- advect: bfloat16 [3, 128, 64, 256], P(None, 'grp', 'slab'), may hold values from -4 to 4
- viscosity: bfloat16 [128, 64, 256], P('grp', 'slab'), may hold values from 0.099609375 to 0.796875
- body_mask: int32 [128, 64, 256], P('grp', 'slab'), may hold values 0 or 1
- marker_x: int32 [2048], replicated, may hold values from 32 to 47
- marker_z: int32 [2048], replicated, may hold values from 0 to 63
- marker_y: int32 [2048], replicated, may hold values from 64 to 191
- drag_weight: float32 [2048], replicated, may hold values from -5 to 5
- inv_x: float32 [128, 128], P(None, 'grp'), may hold values from 0 to 1, as said below
- inv_y: float32 [256, 256], replicated, may hold values from 0 to 1, as said below
- inv_z: float32 [64, 64], replicated, may hold values from 0 to 1, as said below
Outputs:
- state_adjoint: float32 [5, 128, 64, 256], P(None, 'grp', 'slab')
The draws below stay inside these ranges and needn't reach their ends.
Inputs may be any that keep to these rules, and one draw needn't show every extreme that they name: `inv_x`: entries of a given inverse. `inv_y`: entries of a given inverse. `inv_z`: entries of a given inverse.
All inputs are finite; a program needn't handle non-finite values. No bound on the sum of `body_mask` on one device may be relied on, other than what follows from the above.
Results may differ from the reference program's by a relative error of at most 0.0003.
Values sent between devices are 32-bit elements; how exact they have to be, the bound alone decides.
A program may use at most 64 MiB of HBM per device.

```python
import math
from functools import partial
import jax
import jax.numpy as jnp
from jax import lax

FIELDS = 5
NY = 256
MARKERS = 2048
NX = 128
NZ = 64


def line_inverse(key, count):
    reach = count / 4.0
    rows_idx = jnp.arange(count)[:, None]
    cols_idx = jnp.arange(count)[None, :]
    apart = jnp.abs(rows_idx - cols_idx).astype(jnp.float32)
    noise = jnp.clip(jax.random.normal(key, (count, count), jnp.float32), -2.0, 2.0) * 0.5
    spread = 0.2 / reach * jnp.exp(-apart / reach) * (1.0 + 0.5 * noise)
    return 0.6 * jnp.eye(count, dtype=jnp.float32) + spread


def draw_inv_x(key, part):
    return line_inverse(jax.random.fold_in(key, 11), NX)


def draw_inv_y(key, part):
    return line_inverse(jax.random.fold_in(key, 23), NY)


def draw_inv_z(key, part):
    return line_inverse(jax.random.fold_in(key, 37), NZ)


def with_ends(values, stream_key, least, largest):
    spot = [jax.random.randint(jax.random.fold_in(stream_key, axis), (), 0, length) for axis, length in enumerate(values.shape)]
    widest = values.shape.index(max(values.shape))
    beside = spot[:widest] + [(spot[widest] + 1) % values.shape[widest]] + spot[widest + 1:]
    return values.at[tuple(spot)].set(least).at[tuple(beside)].set(largest)


def block_levels(stream_key, extent, shards, least, top_value):
    loudness = 1.0
    for axis_at, shards_of in shards:
        draws = jax.random.uniform(jax.random.fold_in(jax.random.fold_in(stream_key, 6), axis_at), (shards_of,), jnp.float32, least / len(shards), top_value / len(shards))
        loudness = loudness * jnp.repeat(jnp.exp(draws), extent[axis_at] // shards_of).reshape((-1,) + (1,) * (len(extent) - 1 - axis_at))
    return loudness


def normal_values(key, dims, scale, limit, pieces=(), kind=jnp.bfloat16):
    values = scale * jax.random.normal(key, dims, jnp.float32)
    if pieces:
        values = values * block_levels(key, dims, pieces, -0.22, 0.18)
    return jnp.clip(values, -limit, limit).astype(kind)


def setup_inputs(seed: int = 0) -> dict:
    splits = jax.random.split(jax.random.key(seed), 12)
    return {
        "adj_out": normal_values(splits[0], (FIELDS, NX, NZ, NY), 1.0, 6.0, ((1, 2), (2, 16)), jnp.float32),
        "advect": normal_values(splits[1], (3, NX, NZ, NY), 1.0, 4.0, ((1, 2), (2, 16))),
        "viscosity": jnp.clip(jnp.exp(math.log(0.796875) - 2.0794415 * jax.random.uniform(splits[2], (NX, NZ, NY), jnp.float32) ** block_levels(splits[2], (NX, NZ, NY), ((0, 2), (1, 16)), -0.2, 0.2)), 0.099609375, 0.796875).astype(jnp.bfloat16),
        "body_mask": with_ends((jax.random.randint(splits[3], (NX, NZ, NY), 0, 10) < 9).astype(jnp.int32), jax.random.fold_in(splits[3], 1), 0, 1),
        "marker_x": with_ends(jax.random.randint(splits[4], (MARKERS,), NX // 4, NX // 4 + NX // 8), jax.random.fold_in(splits[4], 1), NX // 4, (NX // 4 + NX // 8) - 1).astype(jnp.int32),
        "marker_z": with_ends(jax.random.randint(splits[5], (MARKERS,), 0, NZ), jax.random.fold_in(splits[5], 1), 0, NZ - 1).astype(jnp.int32),
        "marker_y": with_ends(jax.random.randint(splits[6], (MARKERS,), NY // 4, 3 * NY // 4), jax.random.fold_in(splits[6], 1), NY // 4, (3 * NY // 4) - 1).astype(jnp.int32),
        "drag_weight": normal_values(splits[7], (MARKERS,), 1.0, 5.0, (), jnp.float32),
        "inv_x": draw_inv_x(jax.random.fold_in(splits[11], 71), 0),
        "inv_y": draw_inv_y(jax.random.fold_in(splits[11], 71), 0),
        "inv_z": draw_inv_z(jax.random.fold_in(splits[11], 71), 0),
    }


time_step = 0.08
highest = lax.Precision.HIGHEST


def adjoint_field(inv_x, inv_y, inv_z, masking, velocity, viscous, field):
    solved = jnp.einsum("jk,xjy->xky", inv_z, field, precision=highest)
    solved = jnp.einsum("jk,xzj->xzk", inv_y, solved, precision=highest)
    solved = jnp.einsum("jk,jzy->kzy", inv_x, solved, precision=highest)
    masked = solved * masking
    padded = jnp.pad(masked, 1)
    centre = padded[1:-1, 1:-1, 1:-1]
    grad_x = (padded[2:, 1:-1, 1:-1] - padded[:-2, 1:-1, 1:-1]) * 0.5
    grad_z = (padded[1:-1, 2:, 1:-1] - padded[1:-1, :-2, 1:-1]) * 0.5
    grad_y = (padded[1:-1, 1:-1, 2:] - padded[1:-1, 1:-1, :-2]) * 0.5
    laplace = (padded[2:, 1:-1, 1:-1] + padded[:-2, 1:-1, 1:-1]
               + padded[1:-1, 2:, 1:-1] + padded[1:-1, :-2, 1:-1]
               + padded[1:-1, 1:-1, 2:] + padded[1:-1, 1:-1, :-2] - 6.0 * centre)
    change = velocity[0] * grad_x + velocity[1] * grad_z + velocity[2] * grad_y + viscous * laplace
    return centre + time_step * change


def reference(adj_out, advect, viscosity, body_mask, marker_x, marker_z, marker_y, drag_weight, inv_x, inv_y, inv_z):
    seeded = adj_out.at[0, marker_x, marker_z, marker_y].add(drag_weight.astype(adj_out.dtype))
    masking = body_mask.astype(adj_out.dtype)
    velocity = advect.astype(adj_out.dtype)
    viscous = viscosity.astype(adj_out.dtype)
    worker = partial(adjoint_field, inv_x, inv_y, inv_z, masking, velocity, viscous)
    return lax.map(worker, seeded)
```

```python
import jax
import jax.numpy as jnp
from jax import lax
from jax.sharding import PartitionSpec as P

time_step = 0.08
highest = lax.Precision.HIGHEST


def neighbours(cells, axis, dim):
    count = lax.axis_size(axis)
    ends = count - 1
    head = lax.slice_in_dim(cells, 0, 1, axis=dim)
    tail = lax.slice_in_dim(cells, cells.shape[dim] - 1, cells.shape[dim], axis=dim)
    before = lax.ppermute(tail, axis, [(i, i + 1) for i in range(ends)])
    after = lax.ppermute(head, axis, [(i + 1, i) for i in range(ends)])
    return before, after


def shifted(cells, before, after, dim):
    size = cells.shape[dim]
    down = jnp.concatenate([before, lax.slice_in_dim(cells, 0, size - 1, axis=dim)], axis=dim)
    up = jnp.concatenate([lax.slice_in_dim(cells, 1, size, axis=dim), after], axis=dim)
    return down, up


def marker_push(shape, marker_x, marker_z, marker_y, drag_weight):
    x_rows, z_rows, y_cells = shape
    local_x = marker_x - lax.axis_index("grp") * x_rows
    local_z = marker_z - lax.axis_index("slab") * z_rows
    inside = (local_x >= 0) & (local_x < x_rows) & (local_z >= 0) & (local_z < z_rows)
    row = jnp.where(inside, local_x * z_rows + local_z, -1)
    at_row = (jnp.arange(x_rows * z_rows)[:, None] == row[None, :]).astype(jnp.float32)
    at_y = jnp.where(marker_y[:, None] == jnp.arange(y_cells)[None, :], drag_weight[:, None], 0.0)
    return jnp.dot(at_row, at_y, precision=highest).reshape(shape)


def to_lines(cells):
    return lax.all_to_all(cells, "slab", split_axis=1, concat_axis=2, tiled=True)


def to_cells(lines):
    return lax.all_to_all(lines, "slab", split_axis=2, concat_axis=1, tiled=True)


def solve_zy(lines, inv_z, inv_y):
    lines = jnp.einsum("jk,cxjy->cxky", inv_z, lines, precision=highest)
    return jnp.einsum("jk,cxzj->cxzk", inv_y, lines, precision=highest)


def solve_x(cells, inv_x):
    return jnp.einsum(
        "jk,cjzy->ckzy", inv_x, lax.all_gather(cells, "grp", axis=1, tiled=True), precision=highest
    )


def body(
    adj_out,
    advect,
    viscosity,
    body_mask,
    marker_x,
    marker_z,
    marker_y,
    drag_weight,
    inv_x,
    inv_y,
    inv_z,
):
    fields, x_rows, z_rows, y_cells = adj_out.shape
    split = fields - fields // 2
    last = adj_out[split:]
    last = solve_x(last, inv_x)
    pushed = marker_push((x_rows, z_rows, y_cells), marker_x, marker_z, marker_y, drag_weight)
    first = adj_out[:split].at[0].add(pushed)
    first = solve_zy(to_lines(first), inv_z, inv_y)
    last = to_lines(last)
    first, last = lax.optimization_barrier((to_cells(first), last))
    last = to_cells(solve_zy(last, inv_z, inv_y))
    first = solve_x(first, inv_x)
    fluid = body_mask.astype(jnp.float32)
    masked = jnp.concatenate([first, last], axis=0) * fluid
    z_before, z_after = neighbours(masked, "slab", 2)
    x_before, x_after = neighbours(masked, "grp", 1)
    x_down, x_up = shifted(masked, x_before, x_after, 1)
    z_down, z_up = shifted(masked, z_before, z_after, 2)
    y_edge = jnp.zeros_like(masked[..., :1])
    y_down, y_up = shifted(masked, y_edge, y_edge, 3)
    grad_x = (x_up - x_down) * 0.5
    grad_z = (z_up - z_down) * 0.5
    grad_y = (y_up - y_down) * 0.5
    laplace = x_up + x_down + z_up + z_down + y_up + y_down - 6.0 * masked
    velocity = advect.astype(jnp.float32)
    viscous = viscosity.astype(jnp.float32)
    change = velocity[0] * grad_x + velocity[1] * grad_z + velocity[2] * grad_y + viscous * laplace
    return masked + time_step * change


def solution(mesh):
    in_specs = (
        P(None, "grp", "slab", None),
        P(None, "grp", "slab", None),
        P("grp", "slab", None),
        P("grp", "slab", None),
        P(),
        P(),
        P(),
        P(),
        P(None, "grp"),
        P(),
        P(),
    )
    out_specs = P(None, "grp", "slab", None)
    return jax.shard_map(body, mesh=mesh, in_specs=in_specs, out_specs=out_specs, check_vma=False)
```

```python
import functools

import jax
import jax.numpy as jnp
from jax import lax
from jax.experimental import pallas as pl
from jax.experimental.pallas import tpu as pltpu
from jax.sharding import PartitionSpec as P

time_step = 0.08
highest = lax.Precision.HIGHEST


def neighbours(cells, axis, dim):
    count = lax.axis_size(axis)
    ends = count - 1
    head = lax.slice_in_dim(cells, 0, 1, axis=dim)
    tail = lax.slice_in_dim(cells, cells.shape[dim] - 1, cells.shape[dim], axis=dim)
    before = lax.ppermute(tail, axis, [(i, i + 1) for i in range(ends)])
    after = lax.ppermute(head, axis, [(i + 1, i) for i in range(ends)])
    return before, after


def shifted(cells, before, after, dim):
    size = cells.shape[dim]
    down = jnp.concatenate([before, lax.slice_in_dim(cells, 0, size - 1, axis=dim)], axis=dim)
    up = jnp.concatenate([lax.slice_in_dim(cells, 1, size, axis=dim), after], axis=dim)
    return down, up


def marker_push(shape, marker_x, marker_z, marker_y, drag_weight):
    x_rows, z_rows, y_cells = shape
    local_x = marker_x - lax.axis_index("grp") * x_rows
    local_z = marker_z - lax.axis_index("slab") * z_rows
    inside = (local_x >= 0) & (local_x < x_rows) & (local_z >= 0) & (local_z < z_rows)
    row = jnp.where(inside, local_x * z_rows + local_z, -1)
    at_row = (jnp.arange(x_rows * z_rows)[:, None] == row[None, :]).astype(jnp.float32)
    at_y = jnp.where(marker_y[:, None] == jnp.arange(y_cells)[None, :], drag_weight[:, None], 0.0)
    return jnp.dot(at_row, at_y, precision=highest).reshape(shape)


def wait_bytes(block, sem):
    pltpu.make_async_copy(block, block, sem).wait()


def send(src, dst, send_sem, recv_sem, axis, to):
    pltpu.make_async_remote_copy(
        src_ref=src,
        dst_ref=dst,
        send_sem=send_sem,
        recv_sem=recv_sem,
        device_id={axis: to},
        device_id_type=pl.DeviceIdType.MESH,
    ).start()


def solve_kernel(
    slabs, grps, cells, mat_x, mat_z, mat_y, out,
    xin, xdone, lines, zdone, ret,
    x_send, x_recv, l_send, l_recv, r_send, r_recv,
):
    fields = cells.shape[0]
    rows = cells.shape[1] * cells.shape[2]
    width = cells.shape[3]
    me = lax.axis_index("slab")
    mine = lax.axis_index("grp")

    barrier = pltpu.get_barrier_semaphore()

    def greet(axis, here, count):
        def one(k, carry):
            pl.semaphore_signal(
                barrier,
                inc=1,
                device_id={axis: lax.rem(here + k, count)},
                device_id_type=pl.DeviceIdType.MESH,
            )
            return carry

        lax.fori_loop(1, count, one, 0)

    greet("slab", me, slabs)
    greet("grp", mine, grps)
    pl.semaphore_wait(barrier, slabs + grps - 2)

    for c in range(fields):
        def to_grp(k, carry):
            send(cells.at[c], xin.at[c, mine], x_send.at[c], x_recv.at[c], "grp", lax.rem(mine + k, grps))
            return carry

        lax.fori_loop(1, grps, to_grp, 0)

    def matmul(left, right):
        return jnp.dot(left, right, precision=highest, preferred_element_type=jnp.float32)

    def x_stage(c):
        xin[c, mine] = cells[c]
        wait_bytes(xin.at[c, pl.ds(0, grps - 1)], x_recv.at[c])
        xdone[c] = matmul(mat_x[...], xin[c].reshape(grps * rows, width)).reshape(cells.shape[1:])
        lines[c, me] = xdone[c, me]

        def to_slab(k, carry):
            d = lax.rem(me + k, slabs)
            send(xdone.at[c, d], lines.at[c, me], l_send.at[c], l_recv.at[c], "slab", d)
            return carry

        lax.fori_loop(1, slabs, to_slab, 0)

    def z_stage(c):
        wait_bytes(lines.at[c, pl.ds(0, slabs - 1)], l_recv.at[c])
        solved = matmul(matmul(mat_z[...], lines[c].reshape(rows, width)), mat_y[...])
        zdone[c] = solved.reshape(cells.shape[1:])
        ret[c, me] = zdone[c, me]

        def to_slab(k, carry):
            d = lax.rem(me + k, slabs)
            send(zdone.at[c, d], ret.at[c, me], r_send.at[c], r_recv.at[c], "slab", d)
            return carry

        lax.fori_loop(1, slabs, to_slab, 0)

    for c in range(fields + 2):
        if c < fields:
            x_stage(c)
        if c >= 2:
            z_stage(c - 2)
    for c in range(fields):
        wait_bytes(ret.at[c, pl.ds(0, slabs - 1)], r_recv.at[c])
        out[c] = ret[c]
    for c in range(fields):
        wait_bytes(xin.at[c, pl.ds(0, grps - 1)], x_send.at[c])
        wait_bytes(lines.at[c, pl.ds(0, slabs - 1)], l_send.at[c])
        wait_bytes(ret.at[c, pl.ds(0, slabs - 1)], r_send.at[c])


def spread(inverse, sources, results):
    rows, columns = inverse.shape
    pick_source = (sources[None, :] == jnp.arange(rows)[:, None]).astype(jnp.float32)
    pick_result = (results[None, :] == jnp.arange(columns)[:, None]).astype(jnp.float32)
    picked = jnp.einsum("jk,kr->rj", inverse, pick_result, precision=highest)
    return jnp.dot(picked, pick_source, precision=highest)


def solve(seeded, inv_x, inv_y, inv_z):
    fields, x_rows, z_rows, width = seeded.shape
    slabs, grps = lax.axis_size("slab"), lax.axis_size("grp")
    x_part = x_rows // slabs
    block = (slabs, x_part * z_rows, width)
    rows = x_rows * z_rows
    at = jnp.arange(rows)
    across = jnp.arange(grps * rows)
    mat_x = spread(inv_x, across // z_rows, at // z_rows)
    mat_x = jnp.where(at[:, None] % z_rows == across[None, :] % z_rows, mat_x, 0.0)
    line_z = at // (x_part * z_rows) * z_rows + at % z_rows
    line_x = at // z_rows % x_part
    mat_z = spread(inv_z, line_z, line_z)
    mat_z = jnp.where(line_x[:, None] == line_x[None, :], mat_z, 0.0)
    whole = pl.BlockSpec(memory_space=pltpu.VMEM)
    sems = pltpu.SemaphoreType.DMA((fields,))
    solved = pl.pallas_call(
        functools.partial(solve_kernel, slabs, grps),
        out_shape=jax.ShapeDtypeStruct((fields,) + block, jnp.float32),
        in_specs=[whole] * 4,
        out_specs=whole,
        scratch_shapes=[
            pltpu.VMEM((fields, grps) + block, jnp.float32),
            pltpu.VMEM((fields,) + block, jnp.float32),
            pltpu.VMEM((fields,) + block, jnp.float32),
            pltpu.VMEM((fields,) + block, jnp.float32),
            pltpu.VMEM((fields,) + block, jnp.float32),
        ]
        + [sems] * 6,
        compiler_params=pltpu.CompilerParams(
            collective_id=0, has_side_effects=True, vmem_limit_bytes=56 * 1024 * 1024
        ),
    )(seeded.reshape((fields,) + block), mat_x, mat_z, inv_y)
    return solved.reshape(seeded.shape)


def body(
    adj_out,
    advect,
    viscosity,
    body_mask,
    marker_x,
    marker_z,
    marker_y,
    drag_weight,
    inv_x,
    inv_y,
    inv_z,
):
    fields, x_rows, z_rows, y_cells = adj_out.shape
    pushed = marker_push((x_rows, z_rows, y_cells), marker_x, marker_z, marker_y, drag_weight)
    solved = solve(adj_out.at[0].add(pushed), inv_x, inv_y, inv_z)
    fluid = body_mask.astype(jnp.float32)
    masked = solved * fluid
    z_before, z_after = neighbours(masked, "slab", 2)
    x_before, x_after = neighbours(masked, "grp", 1)
    x_down, x_up = shifted(masked, x_before, x_after, 1)
    z_down, z_up = shifted(masked, z_before, z_after, 2)
    y_edge = jnp.zeros_like(masked[..., :1])
    y_down, y_up = shifted(masked, y_edge, y_edge, 3)
    grad_x = (x_up - x_down) * 0.5
    grad_z = (z_up - z_down) * 0.5
    grad_y = (y_up - y_down) * 0.5
    laplace = x_up + x_down + z_up + z_down + y_up + y_down - 6.0 * masked
    velocity = advect.astype(jnp.float32)
    viscous = viscosity.astype(jnp.float32)
    change = velocity[0] * grad_x + velocity[1] * grad_z + velocity[2] * grad_y + viscous * laplace
    return masked + time_step * change


def solution(mesh):
    in_specs = (
        P(None, "grp", "slab", None),
        P(None, "grp", "slab", None),
        P("grp", "slab", None),
        P("grp", "slab", None),
        P(),
        P(),
        P(),
        P(),
        P(None, "grp"),
        P(),
        P(),
    )
    out_specs = P(None, "grp", "slab", None)
    return jax.shard_map(body, mesh=mesh, in_specs=in_specs, out_specs=out_specs, check_vma=False)
```

```python
import functools

import jax
import jax.numpy as jnp
from jax import lax
from jax.experimental import pallas as pl
from jax.experimental.pallas import tpu as pltpu
from jax.sharding import PartitionSpec as P

time_step = 0.08
highest = lax.Precision.HIGHEST


def shifted(cells, before, after, dim):
    size = cells.shape[dim]
    down = jnp.concatenate([before, lax.slice_in_dim(cells, 0, size - 1, axis=dim)], axis=dim)
    up = jnp.concatenate([lax.slice_in_dim(cells, 1, size, axis=dim), after], axis=dim)
    return down, up


def marker_push(shape, marker_x, marker_z, marker_y, drag_weight):
    x_rows, z_rows, y_cells = shape
    local_x = marker_x - lax.axis_index("grp") * x_rows
    local_z = marker_z - lax.axis_index("slab") * z_rows
    inside = (local_x >= 0) & (local_x < x_rows) & (local_z >= 0) & (local_z < z_rows)
    row = jnp.where(inside, local_x * z_rows + local_z, -1)
    at_row = (jnp.arange(x_rows * z_rows)[:, None] == row[None, :]).astype(jnp.float32)
    at_y = jnp.where(marker_y[:, None] == jnp.arange(y_cells)[None, :], drag_weight[:, None], 0.0)
    return jnp.dot(at_row, at_y, precision=highest).reshape(shape)


def wait_bytes(block, sem):
    pltpu.make_async_copy(block, block, sem).wait()


def send(src, dst, send_sem, recv_sem, axis, to):
    pltpu.make_async_remote_copy(
        src_ref=src,
        dst_ref=dst,
        send_sem=send_sem,
        recv_sem=recv_sem,
        device_id={axis: to},
        device_id_type=pl.DeviceIdType.MESH,
    ).start()


def solve_kernel(
    slabs, grps, z_rows, cells, fluid, mat_x, mat_z, mat_y,
    out, z_before, z_after, x_before, x_after,
    xin, xdone, lines, zdone, ret, z_faces, x_faces, z_halo, x_halo,
    x_send, x_recv, l_send, l_recv, r_send, r_recv, h_send, h_recv,
):
    fields = cells.shape[0]
    rows = cells.shape[1] * cells.shape[2]
    width = cells.shape[3]
    me = lax.axis_index("slab")
    mine = lax.axis_index("grp")

    barrier = pltpu.get_barrier_semaphore()

    def greet(axis, here, count):
        def one(k, carry):
            pl.semaphore_signal(
                barrier,
                inc=1,
                device_id={axis: lax.rem(here + k, count)},
                device_id_type=pl.DeviceIdType.MESH,
            )
            return carry

        lax.fori_loop(1, count, one, 0)

    greet("slab", me, slabs)
    greet("grp", mine, grps)
    pl.semaphore_wait(barrier, slabs + grps - 2)

    for c in range(fields):
        def to_grp(k, carry):
            send(cells.at[c], xin.at[c, mine], x_send.at[c], x_recv.at[c], "grp", lax.rem(mine + k, grps))
            return carry

        lax.fori_loop(1, grps, to_grp, 0)

    def matmul(left, right):
        return jnp.dot(left, right, precision=highest, preferred_element_type=jnp.float32)

    def x_stage(c):
        xin[c, mine] = cells[c]
        wait_bytes(xin.at[c, pl.ds(0, grps - 1)], x_recv.at[c])
        xdone[c] = matmul(mat_x[...], xin[c].reshape(grps * rows, width)).reshape(cells.shape[1:])
        lines[c, me] = xdone[c, me]

        def to_slab(k, carry):
            d = lax.rem(me + k, slabs)
            send(xdone.at[c, d], lines.at[c, me], l_send.at[c], l_recv.at[c], "slab", d)
            return carry

        lax.fori_loop(1, slabs, to_slab, 0)

    def z_stage(c):
        wait_bytes(lines.at[c, pl.ds(0, slabs - 1)], l_recv.at[c])
        solved = matmul(matmul(mat_z[...], lines[c].reshape(rows, width)), mat_y[...])
        zdone[c] = solved.reshape(cells.shape[1:])
        ret[c, me] = zdone[c, me]

        def to_slab(k, carry):
            d = lax.rem(me + k, slabs)
            send(zdone.at[c, d], ret.at[c, me], r_send.at[c], r_recv.at[c], "slab", d)
            return carry

        lax.fori_loop(1, slabs, to_slab, 0)

    block_rows = cells.shape[2]
    x_part = block_rows // z_rows

    def halos(c):
        return (
            (z_faces.at[c, 0], z_halo.at[c, 0], "slab", lax.rem(me + 1, slabs)),
            (z_faces.at[c, 1], z_halo.at[c, 1], "slab", lax.rem(me + slabs - 1, slabs)),
            (x_faces.at[c, 0], x_halo.at[c, 0], "grp", lax.rem(mine + 1, grps)),
            (x_faces.at[c, 1], x_halo.at[c, 1], "grp", lax.rem(mine + grps - 1, grps)),
        )

    def mask_stage(c):
        wait_bytes(ret.at[c, pl.ds(0, slabs - 1)], r_recv.at[c])
        out[c] = ret[c] * fluid[...]
        for i in range(x_part):
            z_faces[c, 0, :, pl.ds(i, 1), :] = out[c, :, pl.ds((i + 1) * z_rows - 1, 1), :]
            z_faces[c, 1, :, pl.ds(i, 1), :] = out[c, :, pl.ds(i * z_rows, 1), :]
        x_faces[c, 0] = out[c, slabs - 1, pl.ds(block_rows - z_rows, z_rows), :]
        x_faces[c, 1] = out[c, 0, pl.ds(0, z_rows), :]
        for h, (src, dst, axis, to) in enumerate(halos(c)):
            send(src, dst, h_send.at[c, h], h_recv.at[c, h], axis, to)

    for c in range(fields + 4):
        if c < fields:
            x_stage(c)
        if 2 <= c < fields + 2:
            z_stage(c - 2)
        if c >= 4:
            mask_stage(c - 4)
    for c in range(fields):
        for h, (src, dst, _, _) in enumerate(halos(c)):
            wait_bytes(dst, h_recv.at[c, h])
            wait_bytes(src, h_send.at[c, h])
        z_before[c] = z_halo[c, 0]
        z_after[c] = z_halo[c, 1]
        x_before[c] = x_halo[c, 0]
        x_after[c] = x_halo[c, 1]
    for c in range(fields):
        wait_bytes(xin.at[c, pl.ds(0, grps - 1)], x_send.at[c])
        wait_bytes(lines.at[c, pl.ds(0, slabs - 1)], l_send.at[c])
        wait_bytes(ret.at[c, pl.ds(0, slabs - 1)], r_send.at[c])


def spread(inverse, sources, results):
    rows, columns = inverse.shape
    pick_source = (sources[None, :] == jnp.arange(rows)[:, None]).astype(jnp.float32)
    pick_result = (results[None, :] == jnp.arange(columns)[:, None]).astype(jnp.float32)
    picked = jnp.einsum("jk,kr->rj", inverse, pick_result, precision=highest)
    return jnp.dot(picked, pick_source, precision=highest)


def solve(seeded, fluid, inv_x, inv_y, inv_z):
    fields, x_rows, z_rows, width = seeded.shape
    slabs, grps = lax.axis_size("slab"), lax.axis_size("grp")
    x_part = x_rows // slabs
    block = (slabs, x_part * z_rows, width)
    rows = x_rows * z_rows
    at = jnp.arange(rows)
    across = jnp.arange(grps * rows)
    mat_x = spread(inv_x, across // z_rows, at // z_rows)
    mat_x = jnp.where(at[:, None] % z_rows == across[None, :] % z_rows, mat_x, 0.0)
    line_z = at // (x_part * z_rows) * z_rows + at % z_rows
    line_x = at // z_rows % x_part
    mat_z = spread(inv_z, line_z, line_z)
    mat_z = jnp.where(line_x[:, None] == line_x[None, :], mat_z, 0.0)
    whole = pl.BlockSpec(memory_space=pltpu.VMEM)
    sems = pltpu.SemaphoreType.DMA((fields,))
    z_face = (slabs, x_part, width)
    x_face = (z_rows, width)
    shapes = [block, z_face, z_face, x_face, x_face]
    masked, z_before, z_after, x_before, x_after = pl.pallas_call(
        functools.partial(solve_kernel, slabs, grps, z_rows),
        out_shape=[jax.ShapeDtypeStruct((fields,) + shape, jnp.float32) for shape in shapes],
        in_specs=[whole] * 5,
        out_specs=[whole] * 5,
        scratch_shapes=[
            pltpu.VMEM((fields, grps) + block, jnp.float32),
            pltpu.VMEM((fields,) + block, jnp.float32),
            pltpu.VMEM((fields,) + block, jnp.float32),
            pltpu.VMEM((fields,) + block, jnp.float32),
            pltpu.VMEM((fields,) + block, jnp.float32),
            pltpu.VMEM((fields, 2) + z_face, jnp.float32),
            pltpu.VMEM((fields, 2) + x_face, jnp.float32),
            pltpu.VMEM((fields, 2) + z_face, jnp.float32),
            pltpu.VMEM((fields, 2) + x_face, jnp.float32),
        ]
        + [sems] * 6
        + [pltpu.SemaphoreType.DMA((fields, 4))] * 2,
        compiler_params=pltpu.CompilerParams(
            collective_id=0, has_side_effects=True, vmem_limit_bytes=56 * 1024 * 1024
        ),
    )(seeded.reshape((fields,) + block), fluid.reshape(block), mat_x, mat_z, inv_y)
    me, mine = lax.axis_index("slab"), lax.axis_index("grp")

    def inner(halo, edge, shape):
        return jnp.where(edge, 0.0, halo.reshape(shape))

    z_shape = (fields, x_rows, 1, width)
    x_shape = (fields, 1, z_rows, width)
    return (
        masked.reshape(seeded.shape),
        inner(z_before, me == 0, z_shape),
        inner(z_after, me == slabs - 1, z_shape),
        inner(x_before, mine == 0, x_shape),
        inner(x_after, mine == grps - 1, x_shape),
    )


def body(
    adj_out,
    advect,
    viscosity,
    body_mask,
    marker_x,
    marker_z,
    marker_y,
    drag_weight,
    inv_x,
    inv_y,
    inv_z,
):
    fields, x_rows, z_rows, y_cells = adj_out.shape
    pushed = marker_push((x_rows, z_rows, y_cells), marker_x, marker_z, marker_y, drag_weight)
    fluid = body_mask.astype(jnp.float32)
    seeded = adj_out.at[0].add(pushed)
    masked, z_before, z_after, x_before, x_after = solve(seeded, fluid, inv_x, inv_y, inv_z)
    x_down, x_up = shifted(masked, x_before, x_after, 1)
    z_down, z_up = shifted(masked, z_before, z_after, 2)
    y_edge = jnp.zeros_like(masked[..., :1])
    y_down, y_up = shifted(masked, y_edge, y_edge, 3)
    grad_x = (x_up - x_down) * 0.5
    grad_z = (z_up - z_down) * 0.5
    grad_y = (y_up - y_down) * 0.5
    laplace = x_up + x_down + z_up + z_down + y_up + y_down - 6.0 * masked
    velocity = advect.astype(jnp.float32)
    viscous = viscosity.astype(jnp.float32)
    change = velocity[0] * grad_x + velocity[1] * grad_z + velocity[2] * grad_y + viscous * laplace
    return masked + time_step * change


def solution(mesh):
    in_specs = (
        P(None, "grp", "slab", None),
        P(None, "grp", "slab", None),
        P("grp", "slab", None),
        P("grp", "slab", None),
        P(),
        P(),
        P(),
        P(),
        P(None, "grp"),
        P(),
        P(),
    )
    out_specs = P(None, "grp", "slab", None)
    return jax.shard_map(body, mesh=mesh, in_specs=in_specs, out_specs=out_specs, check_vma=False)
```

```python
import functools

import jax
import jax.numpy as jnp
from jax import lax
from jax.experimental import pallas as pl
from jax.experimental.pallas import tpu as pltpu
from jax.sharding import PartitionSpec as P

time_step = 0.08
highest = lax.Precision.HIGHEST


def shifted(cells, before, after, dim):
    size = cells.shape[dim]
    down = jnp.concatenate([before, lax.slice_in_dim(cells, 0, size - 1, axis=dim)], axis=dim)
    up = jnp.concatenate([lax.slice_in_dim(cells, 1, size, axis=dim), after], axis=dim)
    return down, up


def marker_push(shape, marker_x, marker_z, marker_y, drag_weight):
    x_rows, z_rows, y_cells = shape
    local_x = marker_x - lax.axis_index("grp") * x_rows
    local_z = marker_z - lax.axis_index("slab") * z_rows
    inside = (local_x >= 0) & (local_x < x_rows) & (local_z >= 0) & (local_z < z_rows)
    row = jnp.where(inside, local_x * z_rows + local_z, -1)
    at_row = (jnp.arange(x_rows * z_rows)[:, None] == row[None, :]).astype(jnp.float32)
    at_y = jnp.where(marker_y[:, None] == jnp.arange(y_cells)[None, :], drag_weight[:, None], 0.0)
    return jnp.dot(at_row, at_y, precision=highest).reshape(shape)


def wait_bytes(block, sem):
    pltpu.make_async_copy(block, block, sem).wait()


def send(src, dst, send_sem, recv_sem, axis, to):
    pltpu.make_async_remote_copy(
        src_ref=src,
        dst_ref=dst,
        send_sem=send_sem,
        recv_sem=recv_sem,
        device_id={axis: to},
        device_id_type=pl.DeviceIdType.MESH,
    ).start()


def solve_kernel(
    slabs, grps, z_rows, cells, fluid, mat_x, mat_z, mat_y,
    out, z_before, z_after, x_before, x_after,
    xin, xdone, lines, zdone, ret, z_faces, x_faces, z_halo, x_halo,
    x_send, x_recv, l_send, l_recv, r_send, r_recv, h_send, h_recv,
):
    fields = cells.shape[0]
    rows = cells.shape[1] * cells.shape[2]
    width = cells.shape[3]
    me = lax.axis_index("slab")
    mine = lax.axis_index("grp")

    barrier = pltpu.get_barrier_semaphore()

    def greet(axis, here, count):
        def one(k, carry):
            pl.semaphore_signal(
                barrier,
                inc=1,
                device_id={axis: lax.rem(here + k, count)},
                device_id_type=pl.DeviceIdType.MESH,
            )
            return carry

        lax.fori_loop(1, count, one, 0)

    greet("slab", me, slabs)
    greet("grp", mine, grps)
    pl.semaphore_wait(barrier, slabs + grps - 2)

    for c in range(fields):
        def to_grp(k, carry):
            send(cells.at[c], xin.at[c, mine], x_send.at[c], x_recv.at[c], "grp", lax.rem(mine + k, grps))
            return carry

        lax.fori_loop(1, grps, to_grp, 0)

    def matmul(left, right):
        return jnp.dot(left, right, precision=highest, preferred_element_type=jnp.float32)

    def x_stage(c):
        xin[c, mine] = cells[c]
        wait_bytes(xin.at[c, pl.ds(0, grps - 1)], x_recv.at[c])
        xdone[c] = matmul(mat_x[...], xin[c].reshape(grps * rows, width)).reshape(cells.shape[1:])
        lines[c, me] = xdone[c, me]

        def to_slab(k, carry):
            d = lax.rem(me + k, slabs)
            send(xdone.at[c, d], lines.at[c, me], l_send.at[c], l_recv.at[c], "slab", d)
            return carry

        lax.fori_loop(1, slabs, to_slab, 0)

    def z_stage(c):
        wait_bytes(lines.at[c, pl.ds(0, slabs - 1)], l_recv.at[c])
        solved = matmul(matmul(mat_z[...], lines[c].reshape(rows, width)), mat_y[...])
        zdone[c] = solved.reshape(cells.shape[1:])
        ret[c, me] = zdone[c, me]

        def to_slab(k, carry):
            d = lax.rem(me + k, slabs)
            send(zdone.at[c, d], ret.at[c, me], r_send.at[c], r_recv.at[c], "slab", d)
            return carry

        lax.fori_loop(1, slabs, to_slab, 0)

    block_rows = cells.shape[2]
    x_part = block_rows // z_rows

    def halos(c):
        return (
            (z_faces.at[c, 0], z_halo.at[c, 0], "slab", lax.rem(me + 1, slabs)),
            (z_faces.at[c, 1], z_halo.at[c, 1], "slab", lax.rem(me + slabs - 1, slabs)),
            (x_faces.at[c, 0], x_halo.at[c, 0], "grp", lax.rem(mine + 1, grps)),
            (x_faces.at[c, 1], x_halo.at[c, 1], "grp", lax.rem(mine + grps - 1, grps)),
        )

    def mask_stage(c):
        wait_bytes(ret.at[c, pl.ds(0, slabs - 1)], r_recv.at[c])
        out[c] = ret[c] * fluid[...]
        for i in range(x_part):
            z_faces[c, 0, :, pl.ds(i, 1), :] = out[c, :, pl.ds((i + 1) * z_rows - 1, 1), :]
            z_faces[c, 1, :, pl.ds(i, 1), :] = out[c, :, pl.ds(i * z_rows, 1), :]
        x_faces[c, 0] = out[c, slabs - 1, pl.ds(block_rows - z_rows, z_rows), :]
        x_faces[c, 1] = out[c, 0, pl.ds(0, z_rows), :]
        for h, (src, dst, axis, to) in enumerate(halos(c)):
            send(src, dst, h_send.at[c, h], h_recv.at[c, h], axis, to)

    for c in range(fields + 2):
        if c < fields:
            x_stage(c)
        if c >= 2:
            z_stage(c - 2)
    for c in range(fields):
        mask_stage(c)
    for c in range(fields):
        for h, (src, dst, _, _) in enumerate(halos(c)):
            wait_bytes(dst, h_recv.at[c, h])
            wait_bytes(src, h_send.at[c, h])
        z_before[c] = z_halo[c, 0]
        z_after[c] = z_halo[c, 1]
        x_before[c] = x_halo[c, 0]
        x_after[c] = x_halo[c, 1]
    for c in range(fields):
        wait_bytes(xin.at[c, pl.ds(0, grps - 1)], x_send.at[c])
        wait_bytes(lines.at[c, pl.ds(0, slabs - 1)], l_send.at[c])
        wait_bytes(ret.at[c, pl.ds(0, slabs - 1)], r_send.at[c])


def spread(inverse, sources, results):
    rows, columns = inverse.shape
    pick_source = (sources[None, :] == jnp.arange(rows)[:, None]).astype(jnp.float32)
    pick_result = (results[None, :] == jnp.arange(columns)[:, None]).astype(jnp.float32)
    picked = jnp.einsum("jk,kr->rj", inverse, pick_result, precision=highest)
    return jnp.dot(picked, pick_source, precision=highest)


def solve(seeded, fluid, inv_x, inv_y, inv_z):
    fields, x_rows, z_rows, width = seeded.shape
    slabs, grps = lax.axis_size("slab"), lax.axis_size("grp")
    x_part = x_rows // slabs
    block = (slabs, x_part * z_rows, width)
    rows = x_rows * z_rows
    at = jnp.arange(rows)
    across = jnp.arange(grps * rows)
    mat_x = spread(inv_x, across // z_rows, at // z_rows)
    mat_x = jnp.where(at[:, None] % z_rows == across[None, :] % z_rows, mat_x, 0.0)
    line_z = at // (x_part * z_rows) * z_rows + at % z_rows
    line_x = at // z_rows % x_part
    mat_z = spread(inv_z, line_z, line_z)
    mat_z = jnp.where(line_x[:, None] == line_x[None, :], mat_z, 0.0)
    whole = pl.BlockSpec(memory_space=pltpu.VMEM)
    sems = pltpu.SemaphoreType.DMA((fields,))
    z_face = (slabs, x_part, width)
    x_face = (z_rows, width)
    shapes = [block, z_face, z_face, x_face, x_face]
    masked, z_before, z_after, x_before, x_after = pl.pallas_call(
        functools.partial(solve_kernel, slabs, grps, z_rows),
        out_shape=[jax.ShapeDtypeStruct((fields,) + shape, jnp.float32) for shape in shapes],
        in_specs=[whole] * 5,
        out_specs=[whole] * 5,
        scratch_shapes=[
            pltpu.VMEM((fields, grps) + block, jnp.float32),
            pltpu.VMEM((fields,) + block, jnp.float32),
            pltpu.VMEM((fields,) + block, jnp.float32),
            pltpu.VMEM((fields,) + block, jnp.float32),
            pltpu.VMEM((fields,) + block, jnp.float32),
            pltpu.VMEM((fields, 2) + z_face, jnp.float32),
            pltpu.VMEM((fields, 2) + x_face, jnp.float32),
            pltpu.VMEM((fields, 2) + z_face, jnp.float32),
            pltpu.VMEM((fields, 2) + x_face, jnp.float32),
        ]
        + [sems] * 6
        + [pltpu.SemaphoreType.DMA((fields, 4))] * 2,
        compiler_params=pltpu.CompilerParams(
            collective_id=0, has_side_effects=True, vmem_limit_bytes=56 * 1024 * 1024
        ),
    )(seeded.reshape((fields,) + block), fluid.reshape(block), mat_x, mat_z, inv_y)
    me, mine = lax.axis_index("slab"), lax.axis_index("grp")

    def inner(halo, edge, shape):
        return jnp.where(edge, 0.0, halo.reshape(shape))

    z_shape = (fields, x_rows, 1, width)
    x_shape = (fields, 1, z_rows, width)
    return (
        masked.reshape(seeded.shape),
        inner(z_before, me == 0, z_shape),
        inner(z_after, me == slabs - 1, z_shape),
        inner(x_before, mine == 0, x_shape),
        inner(x_after, mine == grps - 1, x_shape),
    )


def body(
    adj_out,
    advect,
    viscosity,
    body_mask,
    marker_x,
    marker_z,
    marker_y,
    drag_weight,
    inv_x,
    inv_y,
    inv_z,
):
    fields, x_rows, z_rows, y_cells = adj_out.shape
    pushed = marker_push((x_rows, z_rows, y_cells), marker_x, marker_z, marker_y, drag_weight)
    fluid = body_mask.astype(jnp.float32)
    seeded = adj_out.at[0].add(pushed)
    masked, z_before, z_after, x_before, x_after = solve(seeded, fluid, inv_x, inv_y, inv_z)
    x_down, x_up = shifted(masked, x_before, x_after, 1)
    z_down, z_up = shifted(masked, z_before, z_after, 2)
    y_edge = jnp.zeros_like(masked[..., :1])
    y_down, y_up = shifted(masked, y_edge, y_edge, 3)
    grad_x = (x_up - x_down) * 0.5
    grad_z = (z_up - z_down) * 0.5
    grad_y = (y_up - y_down) * 0.5
    laplace = x_up + x_down + z_up + z_down + y_up + y_down - 6.0 * masked
    velocity = advect.astype(jnp.float32)
    viscous = viscosity.astype(jnp.float32)
    change = velocity[0] * grad_x + velocity[1] * grad_z + velocity[2] * grad_y + viscous * laplace
    return masked + time_step * change


def solution(mesh):
    in_specs = (
        P(None, "grp", "slab", None),
        P(None, "grp", "slab", None),
        P("grp", "slab", None),
        P("grp", "slab", None),
        P(),
        P(),
        P(),
        P(),
        P(None, "grp"),
        P(),
        P(),
    )
    out_specs = P(None, "grp", "slab", None)
    return jax.shard_map(body, mesh=mesh, in_specs=in_specs, out_specs=out_specs, check_vma=False)
```

```python
import functools

import jax
import jax.numpy as jnp
from jax import lax
from jax.experimental import pallas as pl
from jax.experimental.pallas import tpu as pltpu
from jax.sharding import PartitionSpec as P

time_step = 0.08
highest = lax.Precision.HIGHEST


def neighbours(cells, axis, dim):
    count = lax.axis_size(axis)
    ends = count - 1
    head = lax.slice_in_dim(cells, 0, 1, axis=dim)
    tail = lax.slice_in_dim(cells, cells.shape[dim] - 1, cells.shape[dim], axis=dim)
    before = lax.ppermute(tail, axis, [(i, i + 1) for i in range(ends)])
    after = lax.ppermute(head, axis, [(i + 1, i) for i in range(ends)])
    return before, after


def shifted(cells, before, after, dim):
    size = cells.shape[dim]
    down = jnp.concatenate([before, lax.slice_in_dim(cells, 0, size - 1, axis=dim)], axis=dim)
    up = jnp.concatenate([lax.slice_in_dim(cells, 1, size, axis=dim), after], axis=dim)
    return down, up


def marker_push(shape, marker_x, marker_z, marker_y, drag_weight):
    x_rows, z_rows, y_cells = shape
    local_x = marker_x - lax.axis_index("grp") * x_rows
    local_z = marker_z - lax.axis_index("slab") * z_rows
    inside = (local_x >= 0) & (local_x < x_rows) & (local_z >= 0) & (local_z < z_rows)
    row = jnp.where(inside, local_x * z_rows + local_z, -1)
    at_row = (jnp.arange(x_rows * z_rows)[:, None] == row[None, :]).astype(jnp.float32)
    at_y = jnp.where(marker_y[:, None] == jnp.arange(y_cells)[None, :], drag_weight[:, None], 0.0)
    return jnp.dot(at_row, at_y, precision=highest).reshape(shape)


def wait_bytes(block, sem):
    pltpu.make_async_copy(block, block, sem).wait()


def send(src, dst, send_sem, recv_sem, axis, to):
    pltpu.make_async_remote_copy(
        src_ref=src,
        dst_ref=dst,
        send_sem=send_sem,
        recv_sem=recv_sem,
        device_id={axis: to},
        device_id_type=pl.DeviceIdType.MESH,
    ).start()


def solve_kernel(
    slabs, grps, cells, mat_x, mat_z, mat_y, out,
    xin, xdone, lines, zdone, ret,
    x_send, x_recv, l_send, l_recv, r_send, r_recv,
):
    fields = cells.shape[0]
    rows = cells.shape[1] * cells.shape[2]
    width = cells.shape[3]
    me = lax.axis_index("slab")
    mine = lax.axis_index("grp")

    barrier = pltpu.get_barrier_semaphore()

    def greet(axis, here, count):
        def one(k, carry):
            pl.semaphore_signal(
                barrier,
                inc=1,
                device_id={axis: lax.rem(here + k, count)},
                device_id_type=pl.DeviceIdType.MESH,
            )
            return carry

        lax.fori_loop(1, count, one, 0)

    greet("slab", me, slabs)
    greet("grp", mine, grps)
    pl.semaphore_wait(barrier, slabs + grps - 2)

    def share_x(src, c):
        def to_grp(k, carry):
            send(src.at[c], xin.at[c, mine], x_send.at[c], x_recv.at[c], "grp", lax.rem(mine + k, grps))
            return carry

        lax.fori_loop(1, grps, to_grp, 0)

    def matmul(left, right):
        return jnp.dot(left, right, precision=highest, preferred_element_type=jnp.float32)

    def solve_x(src, c):
        xin[c, mine] = src[c]
        wait_bytes(xin.at[c, pl.ds(0, grps - 1)], x_recv.at[c])
        return matmul(mat_x[...], xin[c].reshape(grps * rows, width)).reshape(cells.shape[1:])

    def x_stage(c):
        if c > 0:
            xdone[c] = solve_x(cells, c)
        ready = xdone if c > 0 else cells
        lines[c, me] = ready[c, me]

        def to_slab(k, carry):
            d = lax.rem(me + k, slabs)
            send(ready.at[c, d], lines.at[c, me], l_send.at[c], l_recv.at[c], "slab", d)
            return carry

        lax.fori_loop(1, slabs, to_slab, 0)

    def z_stage(c):
        wait_bytes(lines.at[c, pl.ds(0, slabs - 1)], l_recv.at[c])
        solved = matmul(matmul(mat_z[...], lines[c].reshape(rows, width)), mat_y[...])
        zdone[c] = solved.reshape(cells.shape[1:])
        ret[c, me] = zdone[c, me]

        def to_slab(k, carry):
            d = lax.rem(me + k, slabs)
            send(zdone.at[c, d], ret.at[c, me], r_send.at[c], r_recv.at[c], "slab", d)
            return carry

        lax.fori_loop(1, slabs, to_slab, 0)

    x_stage(0)
    for c in range(1, fields):
        share_x(cells, c)
    for c in range(1, fields + 2):
        if c < fields:
            x_stage(c)
        if c >= 2:
            z_stage(c - 2)
        if c == fields:
            wait_bytes(ret.at[0, pl.ds(0, slabs - 1)], r_recv.at[0])
            share_x(ret, 0)
    out[0] = solve_x(ret, 0)
    for c in range(1, fields):
        wait_bytes(ret.at[c, pl.ds(0, slabs - 1)], r_recv.at[c])
        out[c] = ret[c]
    for c in range(fields):
        wait_bytes(xin.at[c, pl.ds(0, grps - 1)], x_send.at[c])
        wait_bytes(lines.at[c, pl.ds(0, slabs - 1)], l_send.at[c])
        wait_bytes(ret.at[c, pl.ds(0, slabs - 1)], r_send.at[c])


def spread(inverse, sources, results):
    rows, columns = inverse.shape
    pick_source = (sources[None, :] == jnp.arange(rows)[:, None]).astype(jnp.float32)
    pick_result = (results[None, :] == jnp.arange(columns)[:, None]).astype(jnp.float32)
    picked = jnp.einsum("jk,kr->rj", inverse, pick_result, precision=highest)
    return jnp.dot(picked, pick_source, precision=highest)


def solve(seeded, inv_x, inv_y, inv_z):
    fields, x_rows, z_rows, width = seeded.shape
    slabs, grps = lax.axis_size("slab"), lax.axis_size("grp")
    x_part = x_rows // slabs
    block = (slabs, x_part * z_rows, width)
    rows = x_rows * z_rows
    at = jnp.arange(rows)
    across = jnp.arange(grps * rows)
    mat_x = spread(inv_x, across // z_rows, at // z_rows)
    mat_x = jnp.where(at[:, None] % z_rows == across[None, :] % z_rows, mat_x, 0.0)
    line_z = at // (x_part * z_rows) * z_rows + at % z_rows
    line_x = at // z_rows % x_part
    mat_z = spread(inv_z, line_z, line_z)
    mat_z = jnp.where(line_x[:, None] == line_x[None, :], mat_z, 0.0)
    whole = pl.BlockSpec(memory_space=pltpu.VMEM)
    sems = pltpu.SemaphoreType.DMA((fields,))
    solved = pl.pallas_call(
        functools.partial(solve_kernel, slabs, grps),
        out_shape=jax.ShapeDtypeStruct((fields,) + block, jnp.float32),
        in_specs=[whole] * 4,
        out_specs=whole,
        scratch_shapes=[
            pltpu.VMEM((fields, grps) + block, jnp.float32),
            pltpu.VMEM((fields,) + block, jnp.float32),
            pltpu.VMEM((fields,) + block, jnp.float32),
            pltpu.VMEM((fields,) + block, jnp.float32),
            pltpu.VMEM((fields,) + block, jnp.float32),
        ]
        + [sems] * 6,
        compiler_params=pltpu.CompilerParams(
            collective_id=0, has_side_effects=True, vmem_limit_bytes=56 * 1024 * 1024
        ),
    )(seeded.reshape((fields,) + block), mat_x, mat_z, inv_y)
    return solved.reshape(seeded.shape)


def body(
    adj_out,
    advect,
    viscosity,
    body_mask,
    marker_x,
    marker_z,
    marker_y,
    drag_weight,
    inv_x,
    inv_y,
    inv_z,
):
    fields, x_rows, z_rows, y_cells = adj_out.shape
    pushed = marker_push((x_rows, z_rows, y_cells), marker_x, marker_z, marker_y, drag_weight)
    solved = solve(adj_out.at[0].add(pushed), inv_x, inv_y, inv_z)
    fluid = body_mask.astype(jnp.float32)
    masked = solved * fluid
    z_before, z_after = neighbours(masked, "slab", 2)
    x_before, x_after = neighbours(masked, "grp", 1)
    x_down, x_up = shifted(masked, x_before, x_after, 1)
    z_down, z_up = shifted(masked, z_before, z_after, 2)
    y_edge = jnp.zeros_like(masked[..., :1])
    y_down, y_up = shifted(masked, y_edge, y_edge, 3)
    grad_x = (x_up - x_down) * 0.5
    grad_z = (z_up - z_down) * 0.5
    grad_y = (y_up - y_down) * 0.5
    laplace = x_up + x_down + z_up + z_down + y_up + y_down - 6.0 * masked
    velocity = advect.astype(jnp.float32)
    viscous = viscosity.astype(jnp.float32)
    change = velocity[0] * grad_x + velocity[1] * grad_z + velocity[2] * grad_y + viscous * laplace
    return masked + time_step * change


def solution(mesh):
    in_specs = (
        P(None, "grp", "slab", None),
        P(None, "grp", "slab", None),
        P("grp", "slab", None),
        P("grp", "slab", None),
        P(),
        P(),
        P(),
        P(),
        P(None, "grp"),
        P(),
        P(),
    )
    out_specs = P(None, "grp", "slab", None)
    return jax.shard_map(body, mesh=mesh, in_specs=in_specs, out_specs=out_specs, check_vma=False)
```
